256 devices in a mesh: seq: 128 (over z_lo, x, y, core), chan: 2 (over z_hi).
Axes of the slice: x: 4, y: 4, z: 8 (z_hi: 2, z_lo: 4; z = z_hi * 4 + z_lo), core: 2. Of those that a mesh axis runs over, the one named last changes fastest.
Arguments:
- projected: float32 [3, 4096, 16384], P(None, 'chan', 'seq'), may hold values from -6 to 6
- short_taps: float32 [3, 4096, 3], P(None, 'chan'), may hold values from -4 to 4
- filters: float32 [4096, 16384], P('chan', 'seq'), may hold values from -1.5 to 1.5
- skip_gain: float32 [4096], P('chan'), may hold values from -4 to 4
- w_out: bfloat16 [4096, 2, 2048], P(None, 'chan', 'seq'), may hold values from -0.09375 to 0.09375
Outputs:
- mixed_out: float32 [16384, 4096], P('seq', 'chan')
The draws below stay inside these ranges and needn't reach their ends.
All inputs are finite; a program needn't handle non-finite values.
Results may differ from the reference program's by a relative error of at most 0.0029.
Values may be sent and summed in bfloat16 or wider, within the bound.
No kernel may reach another device: no remote copies, remote signals or barrier semaphores. Data moves between devices by JAX's collectives and lax.ppermute only.
A program may use at most 128 MiB of HBM per device.

```python
import jax
import jax.numpy as jnp
from jax import lax

CH = 4096
D = 4096
LENGTH = 16384
N_CHAN = 2


def draw_filters(key, part):
    key = jax.random.fold_in(key, 7)
    keys = jax.random.split(key, 5)
    position = jnp.arange(LENGTH, dtype=jnp.float32)[None, :]
    noise = jnp.clip(jax.random.normal(keys[0], (CH, LENGTH), jnp.float32), -5.0, 5.0)
    slow_share = 0.5
    slow = jax.random.uniform(keys[1], (CH, 1), jnp.float32) < slow_share
    spread = jax.random.uniform(keys[2], (CH, 1), jnp.float32)
    slow_rate = jnp.exp(jnp.log(0.2 / LENGTH) + spread * jnp.log(10.0))
    fast_low = jnp.log(8.0 / LENGTH)
    fast_rate = jnp.exp(fast_low + spread * (jnp.log(1.0 / 30.0) - fast_low))
    rate = jnp.where(slow, slow_rate, fast_rate)
    envelope = jnp.exp(-rate * position)
    starts = jax.random.randint(keys[3], (4,), 0, LENGTH)
    factors = jax.random.uniform(keys[4], (4,), jnp.float32, 0.5, 0.8)
    for index in range(4):
        envelope = envelope * jnp.where(position >= starts[index].astype(jnp.float32), factors[index], 1.0)
    energy = jnp.expm1(-2.0 * rate * LENGTH) / jnp.expm1(-2.0 * rate)
    return (noise * envelope / jnp.sqrt(energy)).astype(jnp.float32)


def levels(own_key, dims, shards, least, high):
    gain = 1.0
    for dim, parts in shards:
        heights = jax.random.uniform(jax.random.fold_in(jax.random.fold_in(own_key, 6), dim), (parts,), jnp.float32, least / len(shards), high / len(shards))
        gain = gain * jnp.repeat(jnp.exp(heights), dims[dim] // parts).reshape((-1,) + (1,) * (len(dims) - 1 - dim))
    return gain


def gaussian(rng, shape, deviation, limit, cuts=(), kind=jnp.bfloat16):
    array = deviation * jax.random.normal(rng, shape, jnp.float32)
    if cuts:
        array = array * levels(rng, shape, cuts, -0.22, 0.18)
    return jnp.clip(array, -limit, limit).astype(kind)


def setup_inputs(seed: int = 0) -> dict:
    streams_of = jax.random.split(jax.random.key(seed), 6)
    projected = gaussian(streams_of[0], (3, CH, LENGTH), 1.0, 6.0, ((1, 2), (2, 128)), jnp.float32)
    short_taps = gaussian(streams_of[1], (3, CH, 3), 0.6, 4.0, ((1, 2),), jnp.float32)
    filters = draw_filters(jax.random.fold_in(streams_of[5], 71), 0)
    skip_gain = gaussian(streams_of[3], (CH,), 1.0, 4.0, ((0, 2),), jnp.float32)
    w_out = gaussian(streams_of[4], (CH, N_CHAN, D // N_CHAN), CH ** -0.5, 0.09375, ((1, 2), (2, 128)))
    return {"projected": projected, "short_taps": short_taps, "filters": filters, "skip_gain": skip_gain, "w_out": w_out}


def short_filter(inputs, taps):
    width = inputs.shape[2]
    padded = jnp.pad(inputs, ((0, 0), (0, 0), (2, 0)))
    return taps[:, :, 0:1] * inputs + taps[:, :, 1:2] * padded[:, :, 1:width + 1] + taps[:, :, 2:3] * padded[:, :, 0:width]


def causal_block(pair):
    signal, kernel = pair
    width = signal.shape[1]
    spec_signal = jnp.fft.rfft(signal, n=2 * width, axis=1)
    spec_kernel = jnp.fft.rfft(kernel, n=2 * width, axis=1)
    return jnp.fft.irfft(spec_signal * spec_kernel, n=2 * width, axis=1)[:, :width].astype(jnp.float32)


def reference(projected, short_taps, filters, skip_gain, w_out):
    mixed = short_filter(projected, short_taps)
    gated = mixed[1] * mixed[2]
    blocks = CH // 256
    convolved = lax.map(causal_block, (gated.reshape(blocks, 256, LENGTH), filters.reshape(blocks, 256, LENGTH)))
    convolved = convolved.reshape(CH, LENGTH)
    features = ((convolved + skip_gain[:, None] * gated) * mixed[0]).astype(jnp.bfloat16)
    weights = w_out.reshape(CH, D)
    return jnp.dot(features.T, weights, preferred_element_type=jnp.float32)
```

```python
import math

import jax
import jax.numpy as jnp
import numpy as np
import ml_dtypes
from jax import lax
from jax.experimental import pallas as pl
from jax.experimental.pallas import tpu as pltpu
from jax.sharding import Mesh, PartitionSpec as P

BLK = 128
SEQ = ("z", "x", "y", "core")
IN_SCALE = 2.0 ** 13
H_SCALE = 2.0 ** 15
f32 = jnp.float32
bf16 = jnp.bfloat16
f16 = jnp.float16


def split_np(m):
    hi = m.astype(np.float32).astype(ml_dtypes.bfloat16)
    lo = (m - hi.astype(np.float64)).astype(np.float32).astype(ml_dtypes.bfloat16)
    return hi, lo


def tables():
    n = BLK * BLK
    k1 = np.arange(BLK)[:, None] + 0.25
    a = np.arange(BLK)[None, :]
    alpha = 2.0 * np.pi * a * k1 / BLK
    fwd_rows = np.concatenate([np.cos(alpha), np.sin(alpha)], axis=0)
    hi, lo = split_np(fwd_rows)
    rows_in = np.concatenate([hi, hi, lo], axis=1)
    tw = 2.0 * np.pi * a * k1 / n
    twiddle = np.concatenate([np.cos(tw), np.sin(tw)], axis=1).astype(np.float32)
    beta = 2.0 * np.pi * ((np.arange(BLK)[:, None] * a) % BLK) / BLK
    c, s = np.cos(beta), np.sin(beta)
    hi, lo = split_np(np.block([[c, s], [-s, c]]))
    cols_in = np.concatenate([hi, hi, lo], axis=0)
    hi, lo = split_np(np.block([[c, -s], [s, c]]))
    cols_out = np.concatenate([hi, hi, lo], axis=0)
    back = np.concatenate([np.cos(alpha).T, np.sin(alpha).T], axis=1) / (n * H_SCALE)
    hi, lo = split_np(back)
    rows_out = np.concatenate([hi, hi, lo], axis=1)
    return rows_in, twiddle, cols_in, cols_out, rows_out


def split(x):
    hi = x.astype(bf16)
    lo = (x - hi.astype(f32)).astype(bf16)
    return hi, lo


def dot(a, b):
    return jnp.dot(a, b, preferred_element_type=f32)


def conv_kernel(rows, width, taps, skip, x, e_in, tw, c_in, c_out, e_out, out, feat):
    lane = lax.broadcasted_iota(jnp.int32, (BLK, BLK), 1)
    row = lax.broadcasted_iota(jnp.int32, (BLK, BLK), 0)
    first = row == 0
    cos, sin = tw[:, :BLK], tw[:, BLK:]

    def back(p, by):
        r = pltpu.roll(p, by, 1)
        s = jnp.where(first, 0.0, pltpu.roll(r, 1, 0))
        return jnp.where(lane < by, s, r)

    def mix(i, c):
        p = x[pl.ds(i * rows + c, BLK, stride=4 * rows), :]
        t = (i * rows + c) * 3
        return taps[t] * p + taps[t + 1] * back(p, 1) + taps[t + 2] * back(p, 2)

    def step(it, carry):
        chans = [it * width + j for j in range(width)]
        gates = []
        pieces = []
        for c in chans:
            gate = mix(1, c) * mix(2, c)
            gates.append(gate)
            pieces += [gate, x[pl.ds(3 * rows + c, BLK, stride=4 * rows), :]]
        hi, lo = split(jnp.concatenate(pieces, axis=1))
        s = dot(e_in[...], jnp.concatenate([hi, lo, hi], axis=0))
        turned = []
        for j in range(2 * width):
            sr = s[:BLK, j * BLK : (j + 1) * BLK]
            si = s[BLK:, j * BLK : (j + 1) * BLK]
            turned.append(jnp.concatenate([sr * cos - si * sin, sr * sin + si * cos], axis=1))
        hi, lo = split(jnp.concatenate(turned, axis=0))
        spec = dot(jnp.concatenate([hi, lo, hi], axis=1), c_in[...])
        prods = []
        for j in range(width):
            g = spec[2 * j * BLK : (2 * j + 1) * BLK]
            h = spec[(2 * j + 1) * BLK : (2 * j + 2) * BLK]
            gr, gi, hr, hm = g[:, :BLK], g[:, BLK:], h[:, :BLK], h[:, BLK:]
            prods.append(jnp.concatenate([gr * hr - gi * hm, gr * hm + gi * hr], axis=1))
        hi, lo = split(jnp.concatenate(prods, axis=0))
        v = dot(jnp.concatenate([hi, lo, hi], axis=1), c_out[...])
        us = []
        for j in range(width):
            vr, vi = v[j * BLK : (j + 1) * BLK, :BLK], v[j * BLK : (j + 1) * BLK, BLK:]
            us.append(jnp.concatenate([vr * cos + vi * sin, vi * cos - vr * sin], axis=0))
        hi, lo = split(jnp.concatenate(us, axis=1))
        y = dot(e_out[...], jnp.concatenate([hi, lo, hi], axis=0))
        for j, c in enumerate(chans):
            f = (y[:, j * BLK : (j + 1) * BLK] + skip[c] * gates[j]) * mix(0, c)
            feat[pl.ds(c, BLK, stride=rows), :] = f
        return carry

    lax.fori_loop(0, rows // width, step, 0)
    done = feat[...].reshape(BLK, rows, BLK).astype(bf16)
    out[0] = done
    out[1] = done


def conv_features(x, taps, skip, rows):
    vmem = pl.BlockSpec(memory_space=pltpu.VMEM)
    smem = pl.BlockSpec(memory_space=pltpu.SMEM)
    consts = [jnp.asarray(t) for t in tables()]
    return pl.pallas_call(
        lambda *refs: conv_kernel(rows, 2, *refs),
        out_shape=jax.ShapeDtypeStruct((2, BLK, rows, BLK), bf16),
        in_specs=[smem, smem] + [vmem] * 6,
        out_specs=vmem,
        scratch_shapes=[pltpu.VMEM((BLK * rows, BLK), f32)],
        compiler_params=pltpu.CompilerParams(vmem_limit_bytes=40 * 2**20),
        name="conv_features",
    )(taps, skip, x.reshape(BLK * 4 * rows, BLK), *consts)


def proj_kernel(own, other, w, out_own, out_other, both):
    @pl.when((pl.program_id(0) == 0) & (pl.program_id(1) == 0))
    def _():
        both[:, :BLK] = own[...]
        both[:, BLK:] = other[...]

    wb = w[...]
    t = dot(wb.reshape(wb.shape[0] * wb.shape[2], wb.shape[3]), both[...])
    out_own[...] = t[:, :BLK].T
    out_other[...] = t[:, BLK:].T


def project(own, other, w):
    chips, halves, cols, depth = w.shape
    per = 8
    whole = pl.BlockSpec((depth, BLK), lambda i, j: (0, 0))
    out = pl.BlockSpec((BLK, per * cols), lambda i, j: (0, i * (chips // per) + j))
    shape = jax.ShapeDtypeStruct((BLK, chips * halves * cols), f32)
    return pl.pallas_call(
        proj_kernel,
        grid=(halves, chips // per),
        out_shape=(shape, shape),
        in_specs=[whole, whole, pl.BlockSpec((per, 1, cols, depth), lambda i, j: (j, i, 0, 0))],
        out_specs=(out, out),
        scratch_shapes=[pltpu.VMEM((depth, 2 * BLK), bf16)],
        compiler_params=pltpu.CompilerParams(vmem_limit_bytes=40 * 2**20),
        name="project",
    )(own, other, w)


def gather_weights(w_out):
    depth = w_out.shape[0]
    wt = w_out.reshape(depth, -1).T
    cols = wt.shape[0]
    z = lax.axis_index("z")
    mine = jnp.zeros((4, cols, depth), bf16)
    for k in range(4):
        pairs = []
        for zs in range(4):
            for cs in range(2):
                i = (zs % 2) * 2 + cs
                pairs.append((zs * 2 + cs, ((i + k) % 4) * 2 + zs // 2))
        part = lax.ppermute(wt, ("z", "core"), pairs)
        mine = lax.dynamic_update_slice(mine, part[None], ((z - k) % 4, 0, 0))
    got = lax.all_gather(mine.reshape(2, 2 * cols, depth), ("x", "y"))
    return got


def body(projected, short_taps, filters, skip_gain, w_out):
    slab, count = filters.shape
    groups = lax.axis_size(SEQ)
    rows = slab // groups
    me = lax.axis_index(SEQ)
    core = lax.axis_index("core")
    w = gather_weights(w_out)
    taps = lax.dynamic_slice(short_taps, (0, me * rows, 0), (3, rows, 3)).reshape(-1) / IN_SCALE
    skip = lax.dynamic_slice(skip_gain, (me * rows,), (rows,))
    p16 = (projected * IN_SCALE).astype(f16).reshape(3, groups, rows, count)
    h16 = (filters * H_SCALE).astype(f16).reshape(1, groups, rows, count)
    packed = jnp.concatenate([p16, h16], axis=0).transpose(1, 0, 2, 3)
    packed = packed.reshape(groups, 4 * rows, count)
    x = lax.all_to_all(packed, SEQ, split_axis=0, concat_axis=0, tiled=True).astype(f32)
    feats = conv_features(x, taps, skip, rows).reshape(2 * groups, rows, count)
    mine = lax.all_to_all(feats, ("chan",) + SEQ, split_axis=0, concat_axis=0, tiled=True)
    mine = mine.reshape(2 * slab, count)
    other = lax.ppermute(mine, "core", [(0, 1), (1, 0)])
    out_own, out_other = project(mine, other, w)
    got = lax.ppermute(out_other, "core", [(0, 1), (1, 0)])
    return jnp.where(
        core == 0,
        jnp.concatenate([out_own, got], axis=1),
        jnp.concatenate([got, out_own], axis=1),
    )


def solution(mesh):
    fine = Mesh(mesh.devices.reshape(4, 4, 4, 2, 2), SEQ + ("chan",))
    in_specs = (
        P(None, "chan", SEQ),
        P(None, "chan", None),
        P("chan", SEQ),
        P("chan"),
        P(None, "chan", SEQ),
    )
    out_specs = P(SEQ, "chan")
    return jax.shard_map(body, mesh=fine, in_specs=in_specs, out_specs=out_specs, check_vma=False)
```

```python
import math

import jax
import jax.numpy as jnp
import numpy as np
import ml_dtypes
from jax import lax
from jax.experimental import pallas as pl
from jax.experimental.pallas import tpu as pltpu
from jax.sharding import Mesh, PartitionSpec as P

BLK = 128
SEQ = ("z", "x", "y", "core")
G_SCALE = 2.0 ** 3
M_SCALE = 2.0 ** 9
H_SCALE = 2.0 ** 15
f32 = jnp.float32
bf16 = jnp.bfloat16
f16 = jnp.float16


def split_np(m):
    hi = m.astype(np.float32).astype(ml_dtypes.bfloat16)
    lo = (m - hi.astype(np.float64)).astype(np.float32).astype(ml_dtypes.bfloat16)
    return hi, lo


def tables():
    n = BLK * BLK
    k1 = np.arange(BLK)[:, None] + 0.25
    a = np.arange(BLK)[None, :]
    alpha = 2.0 * np.pi * a * k1 / BLK
    fwd_rows = np.concatenate([np.cos(alpha), np.sin(alpha)], axis=0)
    hi, lo = split_np(fwd_rows)
    rows_in = np.concatenate([hi, hi, lo], axis=1)
    tw = 2.0 * np.pi * a * k1 / n
    twiddle = np.concatenate([np.cos(tw), np.sin(tw)], axis=1).astype(np.float32)
    beta = 2.0 * np.pi * ((np.arange(BLK)[:, None] * a) % BLK) / BLK
    c, s = np.cos(beta), np.sin(beta)
    hi, lo = split_np(np.block([[c, s], [-s, c]]))
    cols_in = np.concatenate([hi, hi, lo], axis=0)
    hi, lo = split_np(np.block([[c, -s], [s, c]]))
    cols_out = np.concatenate([hi, hi, lo], axis=0)
    back = np.concatenate([np.cos(alpha).T, np.sin(alpha).T], axis=1) / (n * H_SCALE * G_SCALE * M_SCALE)
    hi, lo = split_np(back)
    rows_out = np.concatenate([hi, hi, lo], axis=1)
    return rows_in, twiddle, cols_in, cols_out, rows_out


def split(x):
    hi = x.astype(bf16)
    lo = (x - hi.astype(f32)).astype(bf16)
    return hi, lo


def dot(a, b):
    return jnp.dot(a, b, preferred_element_type=f32)


def edge_kernel(p, out):
    lane = lax.broadcasted_iota(jnp.int32, (BLK, BLK), 1)
    for q in range(0, p.shape[1], BLK):
        x = [p[i, q : q + BLK, :] for i in range(3)]
        x = [pltpu.roll(x[0], BLK - 4, 1), pltpu.roll(x[1], BLK - 2, 1), x[2]]
        t = jnp.where(lane < BLK - 4, x[0], jnp.where(lane < BLK - 2, x[1], x[2]))
        out[:, q : q + BLK] = t.T[BLK - 8 :]


def edges(projected):
    slab = projected.shape[1]
    per = slab // 4
    return pl.pallas_call(
        edge_kernel,
        grid=(4,),
        out_shape=jax.ShapeDtypeStruct((8, slab), f32),
        in_specs=[pl.BlockSpec((3, per, BLK), lambda i: (0, i, 0))],
        out_specs=pl.BlockSpec((8, per), lambda i: (0, i)),
        name="edges",
    )(projected)


def spread_table():
    e = np.zeros((32, 15, BLK), np.float32)
    for i in range(3):
        for j in range(3):
            e[8 + 8 * i + j, 3 * i + j, :] = 1.0
        e[2 * i + 3, 9 + i, 0] = 1.0
        e[2 * i + 2, 12 + i, 0] = 1.0
        e[2 * i + 3, 12 + i, 1] = 1.0
    e = e.reshape(32, 15 * BLK)
    return np.concatenate([e, e, e], axis=0).astype(ml_dtypes.bfloat16)


def gate_kernel(rows, p, halo, taps, h, table, out):
    lane = lax.broadcasted_iota(jnp.int32, (BLK, BLK), 1)
    group = BLK // rows
    left = jnp.concatenate([halo[...], taps[0], taps[1], taps[2]], axis=0)
    parts = []
    for k in range(3):
        parts.append(left.astype(bf16))
        left = left - parts[-1].astype(f32)
    cols = jnp.concatenate(parts, axis=0)
    shape = (group, rows, BLK)
    for it in range(h.shape[0] // BLK):
        sl = slice(it * BLK, (it + 1) * BLK)
        wide = lax.dot_general(
            cols[:, sl], table[...], (((0,), (0,)), ((), ())), preferred_element_type=f32
        )
        col = [wide[:, j * BLK : (j + 1) * BLK] for j in range(15)]
        mixed = []
        for i in range(3):
            x = p[i, sl, :]
            x1 = jnp.where(lane < 1, col[9 + i], pltpu.roll(x, 1, 1))
            x2 = jnp.where(lane < 2, col[12 + i], pltpu.roll(x, 2, 1))
            mixed.append(col[3 * i] * x + col[3 * i + 1] * x1 + col[3 * i + 2] * x2)
        dst = slice(it * group, (it + 1) * group)
        out[dst, 0:rows, :] = (mixed[1] * mixed[2] * G_SCALE).reshape(shape)
        out[dst, rows : 2 * rows, :] = (h[sl, :] * H_SCALE).reshape(shape)
        out[dst, 2 * rows : 3 * rows, :] = (mixed[0] * M_SCALE).reshape(shape)


def gate_pack(projected, halo, taps, filters, rows):
    slab, count = filters.shape
    steps = 8
    per = slab // steps
    table = jnp.asarray(spread_table())
    return pl.pallas_call(
        lambda *refs: gate_kernel(rows, *refs),
        grid=(steps,),
        out_shape=jax.ShapeDtypeStruct((slab // rows, 3 * rows, count), f32),
        in_specs=[
            pl.BlockSpec((3, per, count), lambda i: (0, i, 0)),
            pl.BlockSpec((8, per), lambda i: (0, i)),
            pl.BlockSpec((3, 8, per), lambda i: (0, 0, i)),
            pl.BlockSpec((per, count), lambda i: (i, 0)),
            pl.BlockSpec(table.shape, lambda i: (0, 0)),
        ],
        out_specs=pl.BlockSpec((per // rows, 3 * rows, count), lambda i: (i, 0, 0)),
        compiler_params=pltpu.CompilerParams(vmem_limit_bytes=16 * 2**20),
        name="gate_pack",
    )(projected, halo, taps, filters, table)


def conv_kernel(rows, width, skip, x, e_in, tw, c_in, c_out, e_out, out, feat):
    cos, sin = tw[:, :BLK], tw[:, BLK:]

    def load(i, c):
        return x[pl.ds(i * rows + c, BLK, stride=3 * rows), :]

    def step(it, carry):
        chans = [it * width + j for j in range(width)]
        gates = []
        pieces = []
        for c in chans:
            gate = load(0, c)
            gates.append(gate)
            pieces += [gate, load(1, c)]
        hi, lo = split(jnp.concatenate(pieces, axis=1))
        s = dot(e_in[...], jnp.concatenate([hi, lo, hi], axis=0))
        turned = []
        for j in range(2 * width):
            sr = s[:BLK, j * BLK : (j + 1) * BLK]
            si = s[BLK:, j * BLK : (j + 1) * BLK]
            turned.append(jnp.concatenate([sr * cos - si * sin, sr * sin + si * cos], axis=1))
        hi, lo = split(jnp.concatenate(turned, axis=0))
        spec = dot(jnp.concatenate([hi, lo, hi], axis=1), c_in[...])
        prods = []
        for j in range(width):
            g = spec[2 * j * BLK : (2 * j + 1) * BLK]
            h = spec[(2 * j + 1) * BLK : (2 * j + 2) * BLK]
            gr, gi, hr, hm = g[:, :BLK], g[:, BLK:], h[:, :BLK], h[:, BLK:]
            prods.append(jnp.concatenate([gr * hr - gi * hm, gr * hm + gi * hr], axis=1))
        hi, lo = split(jnp.concatenate(prods, axis=0))
        v = dot(jnp.concatenate([hi, lo, hi], axis=1), c_out[...])
        us = []
        for j in range(width):
            vr, vi = v[j * BLK : (j + 1) * BLK, :BLK], v[j * BLK : (j + 1) * BLK, BLK:]
            us.append(jnp.concatenate([vr * cos + vi * sin, vi * cos - vr * sin], axis=0))
        hi, lo = split(jnp.concatenate(us, axis=1))
        y = dot(e_out[...], jnp.concatenate([hi, lo, hi], axis=0))
        for j, c in enumerate(chans):
            f = (y[:, j * BLK : (j + 1) * BLK] + skip[c] * gates[j]) * load(2, c)
            feat[pl.ds(c, BLK, stride=rows), :] = f
        return carry

    lax.fori_loop(0, rows // width, step, 0)
    done = feat[...].reshape(BLK, rows, BLK).astype(bf16)
    out[0] = done
    out[1] = done


def conv_features(x, skip, rows):
    vmem = pl.BlockSpec(memory_space=pltpu.VMEM)
    smem = pl.BlockSpec(memory_space=pltpu.SMEM)
    consts = [jnp.asarray(t) for t in tables()]
    return pl.pallas_call(
        lambda *refs: conv_kernel(rows, 8, *refs),
        out_shape=jax.ShapeDtypeStruct((2, BLK, rows, BLK), bf16),
        in_specs=[smem] + [vmem] * 6,
        out_specs=vmem,
        scratch_shapes=[pltpu.VMEM((BLK * rows, BLK), f32)],
        compiler_params=pltpu.CompilerParams(vmem_limit_bytes=20 * 2**20),
        cost_estimate=pl.CostEstimate(flops=4 * 10**9, bytes_accessed=6 * 10**6, transcendentals=0),
        name="conv_features",
    )(skip, x.reshape(BLK * 3 * rows, BLK), *consts)


def spread(w_out):
    wt = w_out.reshape(w_out.shape[0], -1).T
    parts = []
    for k in range(4):
        pairs = []
        for zs in range(4):
            for cs in range(2):
                i = (zs % 2) * 2 + cs
                pairs.append((zs * 2 + cs, ((i + k) % 4) * 2 + zs // 2))
        parts.append(lax.ppermute(wt, ("z", "core"), pairs))
    return parts


def proj_kernel(_, own, other, wa, wb, out_own, out_other, both):
    @pl.when((pl.program_id(0) == 0) & (pl.program_id(1) == 0))
    def _():
        both[:, :BLK] = own[...]
        both[:, BLK:] = other[...]

    w = jnp.concatenate([wa[...], wb[...]], axis=1)
    t = dot(w.reshape(-1, w.shape[3]), both[...])
    out_own[...] = t[:, :BLK].T
    out_other[...] = t[:, BLK:].T


def project(pos, own, other, w):
    chips, parts, cols, depth = w.shape
    per = 8
    whole = pl.BlockSpec((depth, BLK), lambda i, j, z: (0, 0))
    out = pl.BlockSpec((BLK, per * 2 * cols), lambda i, j, z: (0, i * (chips // per) + j))
    shape = jax.ShapeDtypeStruct((BLK, chips * parts * cols), f32)

    def pick(c):
        return pl.BlockSpec(
            (per, 1, cols, depth), lambda i, j, z: (j, lax.rem(z[0] + 4 - (2 * i + c), 4), 0, 0)
        )

    return pl.pallas_call(
        proj_kernel,
        grid_spec=pltpu.PrefetchScalarGridSpec(
            num_scalar_prefetch=1,
            grid=(2, chips // per),
            in_specs=[whole, whole, pick(0), pick(1)],
            out_specs=[out, out],
            scratch_shapes=[pltpu.VMEM((depth, 2 * BLK), bf16)],
        ),
        out_shape=(shape, shape),
        compiler_params=pltpu.CompilerParams(vmem_limit_bytes=32 * 2**20),
        name="project",
    )(pos, own, other, w, w)


def body(projected, short_taps, filters, skip_gain, w_out):
    slab, count = filters.shape
    groups = lax.axis_size(SEQ)
    rows = slab // groups
    me = lax.axis_index(SEQ)
    core = lax.axis_index("core")
    skip = lax.dynamic_slice(skip_gain, (me * rows,), (rows,)) / (G_SCALE * M_SCALE)
    last = edges(projected)
    last, w_out = lax.optimization_barrier((last, w_out))
    halo = lax.ppermute(last, SEQ, [(i, i + 1) for i in range(groups - 1)])
    parts = spread(w_out)
    taps = jnp.pad(short_taps.transpose(0, 2, 1), ((0, 0), (0, 5), (0, 0)))
    packed = gate_pack(projected, halo, taps, filters, rows).astype(f16)
    packed, parts = lax.optimization_barrier((packed, parts))
    w = lax.all_gather(jnp.stack(parts), ("x", "y"))
    w = w.reshape(-1, 4, w.shape[-2], w.shape[-1])
    x = lax.all_to_all(packed, SEQ, split_axis=0, concat_axis=0, tiled=True)
    feats = conv_features(x.astype(f32), skip, rows).reshape(2 * groups, rows, count)
    mine = lax.all_to_all(feats, ("chan",) + SEQ, split_axis=0, concat_axis=0, tiled=True)
    mine = mine.reshape(2 * slab, count)
    swap = [(0, 1), (1, 0)]
    other = lax.ppermute(mine, "core", swap)
    out_own, out_other = project(lax.axis_index("z").reshape(1), mine, other, w)
    got = lax.ppermute(out_other, "core", swap)
    return jnp.where(
        core == 0,
        jnp.concatenate([out_own, got], axis=1),
        jnp.concatenate([got, out_own], axis=1),
    )


def solution(mesh):
    fine = Mesh(mesh.devices.reshape(4, 4, 4, 2, 2), SEQ + ("chan",))
    in_specs = (
        P(None, "chan", SEQ),
        P(None, "chan", None),
        P("chan", SEQ),
        P("chan"),
        P(None, "chan", SEQ),
    )
    out_specs = P(SEQ, "chan")
    return jax.shard_map(body, mesh=fine, in_specs=in_specs, out_specs=out_specs, check_vma=False)
```

```python
import math

import jax
import jax.numpy as jnp
import numpy as np
import ml_dtypes
from jax import lax
from jax.experimental import pallas as pl
from jax.experimental.pallas import tpu as pltpu
from jax.sharding import Mesh, PartitionSpec as P

BLK = 128
SEQ = ("z", "x", "y", "core")
G_SCALE = 2.0 ** 3
M_SCALE = 2.0 ** 9
H_SCALE = 2.0 ** 15
f32 = jnp.float32
bf16 = jnp.bfloat16
f16 = jnp.float16


def split_np(m):
    hi = m.astype(np.float32).astype(ml_dtypes.bfloat16)
    lo = (m - hi.astype(np.float64)).astype(np.float32).astype(ml_dtypes.bfloat16)
    return hi, lo


def tables():
    n = BLK * BLK
    k1 = np.arange(BLK)[:, None] + 0.25
    a = np.arange(BLK)[None, :]
    alpha = 2.0 * np.pi * a * k1 / BLK
    fwd_rows = np.concatenate([np.cos(alpha), np.sin(alpha)], axis=0)
    hi, lo = split_np(fwd_rows)
    rows_in = np.concatenate([hi, hi, lo], axis=1)
    tw = 2.0 * np.pi * a * k1 / n
    twiddle = np.concatenate([np.cos(tw), np.sin(tw)], axis=1).astype(np.float32)
    beta = 2.0 * np.pi * ((np.arange(BLK)[:, None] * a) % BLK) / BLK
    c, s = np.cos(beta), np.sin(beta)
    hi, lo = split_np(np.block([[c, s], [-s, c]]))
    cols_in = np.concatenate([hi, hi, lo], axis=0)
    hi, lo = split_np(np.block([[c, -s], [s, c]]))
    cols_out = np.concatenate([hi, hi, lo], axis=0)
    back = np.concatenate([np.cos(alpha).T, np.sin(alpha).T], axis=1) / (n * H_SCALE * G_SCALE * M_SCALE)
    hi, lo = split_np(back)
    rows_out = np.concatenate([hi, hi, lo], axis=1)
    return rows_in, twiddle, cols_in, cols_out, rows_out


def split(x):
    hi = x.astype(bf16)
    lo = (x - hi.astype(f32)).astype(bf16)
    return hi, lo


def dot(a, b):
    return jnp.dot(a, b, preferred_element_type=f32)


def edge_kernel(p, out):
    lane = lax.broadcasted_iota(jnp.int32, (BLK, BLK), 1)
    for q in range(0, p.shape[1], BLK):
        x = [p[i, q : q + BLK, :] for i in range(3)]
        x = [pltpu.roll(x[0], BLK - 4, 1), pltpu.roll(x[1], BLK - 2, 1), x[2]]
        t = jnp.where(lane < BLK - 4, x[0], jnp.where(lane < BLK - 2, x[1], x[2]))
        out[:, q : q + BLK] = t.T[BLK - 8 :]


def edges(projected):
    vmem = pl.BlockSpec(memory_space=pltpu.VMEM)
    return pl.pallas_call(
        edge_kernel,
        out_shape=jax.ShapeDtypeStruct((8, projected.shape[1]), f32),
        in_specs=[vmem],
        out_specs=vmem,
        name="edges",
    )(projected)


def spread_table():
    e = np.zeros((32, 15, BLK), np.float32)
    for i in range(3):
        for j in range(3):
            e[8 + 8 * i + j, 3 * i + j, :] = 1.0
        e[2 * i + 3, 9 + i, 0] = 1.0
        e[2 * i + 2, 12 + i, 0] = 1.0
        e[2 * i + 3, 12 + i, 1] = 1.0
    e = e.reshape(32, 15 * BLK)
    return np.concatenate([e, e, e], axis=0).astype(ml_dtypes.bfloat16)


def gate_kernel(rows, p, halo, taps, h, table, out, left_ref):
    lane = lax.broadcasted_iota(jnp.int32, (BLK, BLK), 1)
    group = BLK // rows
    left_ref[0:8, :] = halo[...]
    left_ref[8:32, :] = jnp.zeros((24, left_ref.shape[1]), f32)
    for i in range(3):
        left_ref[8 + 8 * i : 11 + 8 * i, :] = taps[i]
    left = left_ref[...]
    parts = []
    for k in range(3):
        parts.append(left.astype(bf16))
        left = left - parts[-1].astype(f32)
    cols = jnp.concatenate(parts, axis=0)
    shape = (group, rows, BLK)
    for it in range(h.shape[0] // BLK):
        sl = slice(it * BLK, (it + 1) * BLK)
        wide = lax.dot_general(
            cols[:, sl], table[...], (((0,), (0,)), ((), ())), preferred_element_type=f32
        )
        col = [wide[:, j * BLK : (j + 1) * BLK] for j in range(15)]
        mixed = []
        for i in range(3):
            x = p[i, sl, :]
            x1 = jnp.where(lane < 1, col[9 + i], pltpu.roll(x, 1, 1))
            x2 = jnp.where(lane < 2, col[12 + i], pltpu.roll(x, 2, 1))
            mixed.append(col[3 * i] * x + col[3 * i + 1] * x1 + col[3 * i + 2] * x2)
        dst = slice(it * group, (it + 1) * group)
        out[dst, 0:rows, :] = (mixed[1] * mixed[2] * G_SCALE).reshape(shape)
        out[dst, rows : 2 * rows, :] = (h[sl, :] * H_SCALE).reshape(shape)
        out[dst, 2 * rows : 3 * rows, :] = (mixed[0] * M_SCALE).reshape(shape)


def gate_pack(projected, halo, taps, filters, rows):
    slab, count = filters.shape
    vmem = pl.BlockSpec(memory_space=pltpu.VMEM)
    return pl.pallas_call(
        lambda *refs: gate_kernel(rows, *refs),
        out_shape=jax.ShapeDtypeStruct((slab // rows, 3 * rows, count), f32),
        in_specs=[vmem] * 5,
        out_specs=vmem,
        scratch_shapes=[pltpu.VMEM((32, slab), f32)],
        compiler_params=pltpu.CompilerParams(vmem_limit_bytes=16 * 2**20),
        cost_estimate=pl.CostEstimate(flops=10**9, bytes_accessed=8 * 10**6, transcendentals=0),
        name="gate_pack",
    )(projected, halo, taps, filters, jnp.asarray(spread_table()))


def conv_kernel(rows, width, skip, x, e_in, tw, c_in, c_out, e_out, out, feat):
    cos, sin = tw[:, :BLK], tw[:, BLK:]

    def load(i, c):
        return x[pl.ds(i * rows + c, BLK, stride=3 * rows), :]

    def step(it, carry):
        chans = [it * width + j for j in range(width)]
        gates = []
        pieces = []
        for c in chans:
            gate = load(0, c)
            gates.append(gate)
            pieces += [gate, load(1, c)]
        hi, lo = split(jnp.concatenate(pieces, axis=1))
        s = dot(e_in[...], jnp.concatenate([hi, lo, hi], axis=0))
        turned = []
        for j in range(2 * width):
            sr = s[:BLK, j * BLK : (j + 1) * BLK]
            si = s[BLK:, j * BLK : (j + 1) * BLK]
            turned.append(jnp.concatenate([sr * cos - si * sin, sr * sin + si * cos], axis=1))
        hi, lo = split(jnp.concatenate(turned, axis=0))
        spec = dot(jnp.concatenate([hi, lo, hi], axis=1), c_in[...])
        prods = []
        for j in range(width):
            g = spec[2 * j * BLK : (2 * j + 1) * BLK]
            h = spec[(2 * j + 1) * BLK : (2 * j + 2) * BLK]
            gr, gi, hr, hm = g[:, :BLK], g[:, BLK:], h[:, :BLK], h[:, BLK:]
            prods.append(jnp.concatenate([gr * hr - gi * hm, gr * hm + gi * hr], axis=1))
        hi, lo = split(jnp.concatenate(prods, axis=0))
        v = dot(jnp.concatenate([hi, lo, hi], axis=1), c_out[...])
        us = []
        for j in range(width):
            vr, vi = v[j * BLK : (j + 1) * BLK, :BLK], v[j * BLK : (j + 1) * BLK, BLK:]
            us.append(jnp.concatenate([vr * cos + vi * sin, vi * cos - vr * sin], axis=0))
        hi, lo = split(jnp.concatenate(us, axis=1))
        y = dot(e_out[...], jnp.concatenate([hi, lo, hi], axis=0))
        for j, c in enumerate(chans):
            f = (y[:, j * BLK : (j + 1) * BLK] + skip[c] * gates[j]) * load(2, c)
            feat[pl.ds(c, BLK, stride=rows), :] = f
        return carry

    lax.fori_loop(0, rows // width, step, 0)
    done = feat[...].reshape(BLK, rows, BLK).astype(bf16)
    out[0] = done
    out[1] = done


def conv_features(x, skip, rows):
    vmem = pl.BlockSpec(memory_space=pltpu.VMEM)
    smem = pl.BlockSpec(memory_space=pltpu.SMEM)
    consts = [jnp.asarray(t) for t in tables()]
    return pl.pallas_call(
        lambda *refs: conv_kernel(rows, 8, *refs),
        out_shape=jax.ShapeDtypeStruct((2, BLK, rows, BLK), bf16),
        in_specs=[smem] + [vmem] * 6,
        out_specs=vmem,
        scratch_shapes=[pltpu.VMEM((BLK * rows, BLK), f32)],
        compiler_params=pltpu.CompilerParams(vmem_limit_bytes=20 * 2**20),
        cost_estimate=pl.CostEstimate(flops=4 * 10**9, bytes_accessed=6 * 10**6, transcendentals=0),
        name="conv_features",
    )(skip, x.reshape(BLK * 3 * rows, BLK), *consts)


def spread(w_out):
    wt = w_out.reshape(w_out.shape[0], -1).T
    parts = []
    for k in range(4):
        pairs = []
        for zs in range(4):
            for cs in range(2):
                i = (zs % 2) * 2 + cs
                pairs.append((zs * 2 + cs, ((i + k) % 4) * 2 + zs // 2))
        parts.append(lax.ppermute(wt, ("z", "core"), pairs))
    return parts


def proj_kernel(_, own, other, wa, wb, out_own, out_other, both):
    @pl.when((pl.program_id(0) == 0) & (pl.program_id(1) == 0))
    def _():
        both[:, :BLK] = own[...]
        both[:, BLK:] = other[...]

    w = jnp.concatenate([wa[...], wb[...]], axis=1)
    t = dot(w.reshape(-1, w.shape[3]), both[...])
    out_own[...] = t[:, :BLK].T
    out_other[...] = t[:, BLK:].T


def project(pos, own, other, w):
    chips, parts, cols, depth = w.shape
    per = 8
    whole = pl.BlockSpec((depth, BLK), lambda i, j, z: (0, 0))
    out = pl.BlockSpec((BLK, per * 2 * cols), lambda i, j, z: (0, i * (chips // per) + j))
    shape = jax.ShapeDtypeStruct((BLK, chips * parts * cols), f32)

    def pick(c):
        return pl.BlockSpec(
            (per, 1, cols, depth), lambda i, j, z: (j, lax.rem(z[0] + 4 - (2 * i + c), 4), 0, 0)
        )

    return pl.pallas_call(
        proj_kernel,
        grid_spec=pltpu.PrefetchScalarGridSpec(
            num_scalar_prefetch=1,
            grid=(2, chips // per),
            in_specs=[whole, whole, pick(0), pick(1)],
            out_specs=[out, out],
            scratch_shapes=[pltpu.VMEM((depth, 2 * BLK), bf16)],
        ),
        out_shape=(shape, shape),
        compiler_params=pltpu.CompilerParams(vmem_limit_bytes=32 * 2**20),
        name="project",
    )(pos, own, other, w, w)


def body(projected, short_taps, filters, skip_gain, w_out):
    slab, count = filters.shape
    groups = lax.axis_size(SEQ)
    rows = slab // groups
    me = lax.axis_index(SEQ)
    core = lax.axis_index("core")
    skip = lax.dynamic_slice(skip_gain, (me * rows,), (rows,)) / (G_SCALE * M_SCALE)
    last = edges(projected)
    last, w_out = lax.optimization_barrier((last, w_out))
    halo = lax.ppermute(last, SEQ, [(i, i + 1) for i in range(groups - 1)])
    parts = spread(w_out)
    taps = short_taps.transpose(0, 2, 1)
    packed = gate_pack(projected, halo, taps, filters, rows).astype(f16)
    packed, parts = lax.optimization_barrier((packed, parts))
    w = lax.all_gather(jnp.stack(parts), ("x", "y"))
    w = w.reshape(-1, 4, w.shape[-2], w.shape[-1])
    x = lax.all_to_all(packed, SEQ, split_axis=0, concat_axis=0, tiled=True)
    feats = conv_features(x.astype(f32), skip, rows).reshape(2 * groups, rows, count)
    mine = lax.all_to_all(feats, ("chan",) + SEQ, split_axis=0, concat_axis=0, tiled=True)
    mine = mine.reshape(2 * slab, count)
    mine, w = lax.optimization_barrier((mine, w))
    swap = [(0, 1), (1, 0)]
    other = lax.ppermute(mine, "core", swap)
    out_own, out_other = project(lax.axis_index("z").reshape(1), mine, other, w)
    got = lax.ppermute(out_other, "core", swap)
    return jnp.where(
        core == 0,
        jnp.concatenate([out_own, got], axis=1),
        jnp.concatenate([got, out_own], axis=1),
    )


def solution(mesh):
    fine = Mesh(mesh.devices.reshape(4, 4, 4, 2, 2), SEQ + ("chan",))
    in_specs = (
        P(None, "chan", SEQ),
        P(None, "chan", None),
        P("chan", SEQ),
        P("chan"),
        P(None, "chan", SEQ),
    )
    out_specs = P(SEQ, "chan")
    return jax.shard_map(body, mesh=fine, in_specs=in_specs, out_specs=out_specs, check_vma=False)
```

```python
import math

import jax
import jax.numpy as jnp
import numpy as np
import ml_dtypes
from jax import lax
from jax.experimental import pallas as pl
from jax.experimental.pallas import tpu as pltpu
from jax.sharding import Mesh, PartitionSpec as P

BLK = 128
SEQ = ("z", "x", "y", "core")
G_SCALE = 2.0 ** 3
M_SCALE = 2.0 ** 9
H_SCALE = 2.0 ** 15
f32 = jnp.float32
bf16 = jnp.bfloat16
f16 = jnp.float16


def split_np(m):
    hi = m.astype(np.float32).astype(ml_dtypes.bfloat16)
    lo = (m - hi.astype(np.float64)).astype(np.float32).astype(ml_dtypes.bfloat16)
    return hi, lo


def tables():
    n = BLK * BLK
    k1 = np.arange(BLK)[:, None] + 0.25
    a = np.arange(BLK)[None, :]
    alpha = 2.0 * np.pi * a * k1 / BLK
    fwd_rows = np.concatenate([np.cos(alpha), np.sin(alpha)], axis=0)
    hi, lo = split_np(fwd_rows)
    rows_in = np.concatenate([hi, hi, lo], axis=1)
    tw = 2.0 * np.pi * a * k1 / n
    twiddle = np.concatenate([np.cos(tw), np.sin(tw)], axis=1).astype(np.float32)
    beta = 2.0 * np.pi * ((np.arange(BLK)[:, None] * a) % BLK) / BLK
    c, s = np.cos(beta), np.sin(beta)
    hi, lo = split_np(np.block([[c, s], [-s, c]]))
    cols_in = np.concatenate([hi, hi, lo], axis=0)
    hi, lo = split_np(np.block([[c, -s], [s, c]]))
    cols_out = np.concatenate([hi, hi, lo], axis=0)
    back = np.concatenate([np.cos(alpha).T, np.sin(alpha).T], axis=1) / (n * H_SCALE * G_SCALE * M_SCALE)
    hi, lo = split_np(back)
    rows_out = np.concatenate([hi, hi, lo], axis=1)
    return rows_in, twiddle, cols_in, cols_out, rows_out


def split(x):
    hi = x.astype(bf16)
    lo = (x - hi.astype(f32)).astype(bf16)
    return hi, lo


def dot(a, b):
    return jnp.dot(a, b, preferred_element_type=f32)


def edge_kernel(p, out):
    lane = lax.broadcasted_iota(jnp.int32, (BLK, BLK), 1)
    for q in range(0, p.shape[1], BLK):
        x = [p[i, q : q + BLK, :] for i in range(3)]
        x = [pltpu.roll(x[0], BLK - 4, 1), pltpu.roll(x[1], BLK - 2, 1), x[2]]
        t = jnp.where(lane < BLK - 4, x[0], jnp.where(lane < BLK - 2, x[1], x[2]))
        out[:, q : q + BLK] = t.T[BLK - 8 :]


def edges(projected):
    vmem = pl.BlockSpec(memory_space=pltpu.VMEM)
    return pl.pallas_call(
        edge_kernel,
        out_shape=jax.ShapeDtypeStruct((8, projected.shape[1]), f32),
        in_specs=[vmem],
        out_specs=vmem,
        name="edges",
    )(projected)


def spread_table():
    e = np.zeros((32, 15, BLK), np.float32)
    for i in range(3):
        for j in range(3):
            e[8 + 8 * i + j, 3 * i + j, :] = 1.0
        e[2 * i + 3, 9 + i, 0] = 1.0
        e[2 * i + 2, 12 + i, 0] = 1.0
        e[2 * i + 3, 12 + i, 1] = 1.0
    e = e.reshape(32, 15 * BLK)
    return np.concatenate([e, e, e], axis=0).astype(ml_dtypes.bfloat16)


def gate_kernel(rows, p, halo, taps, h, table, out, left_ref):
    lane = lax.broadcasted_iota(jnp.int32, (BLK, BLK), 1)
    group = BLK // rows
    left_ref[0:8, :] = halo[...]
    left_ref[8:32, :] = jnp.zeros((24, left_ref.shape[1]), f32)
    for i in range(3):
        left_ref[8 + 8 * i : 11 + 8 * i, :] = taps[i]
    left = left_ref[...]
    parts = []
    for k in range(3):
        parts.append(left.astype(bf16))
        left = left - parts[-1].astype(f32)
    cols = jnp.concatenate(parts, axis=0)
    shape = (group, rows, BLK)
    for it in range(h.shape[0] // BLK):
        sl = slice(it * BLK, (it + 1) * BLK)
        wide = lax.dot_general(
            cols[:, sl], table[...], (((0,), (0,)), ((), ())), preferred_element_type=f32
        )
        col = [wide[:, j * BLK : (j + 1) * BLK] for j in range(15)]
        mixed = []
        for i in range(3):
            x = p[i, sl, :]
            x1 = jnp.where(lane < 1, col[9 + i], pltpu.roll(x, 1, 1))
            x2 = jnp.where(lane < 2, col[12 + i], pltpu.roll(x, 2, 1))
            mixed.append(col[3 * i] * x + col[3 * i + 1] * x1 + col[3 * i + 2] * x2)
        dst = slice(it * group, (it + 1) * group)
        out[dst, 0:rows, :] = (mixed[1] * mixed[2] * G_SCALE).reshape(shape)
        out[dst, rows : 2 * rows, :] = (h[sl, :] * H_SCALE).reshape(shape)
        out[dst, 2 * rows : 3 * rows, :] = (mixed[0] * M_SCALE).reshape(shape)


def gate_pack(projected, halo, taps, filters, rows):
    slab, count = filters.shape
    vmem = pl.BlockSpec(memory_space=pltpu.VMEM)
    return pl.pallas_call(
        lambda *refs: gate_kernel(rows, *refs),
        out_shape=jax.ShapeDtypeStruct((slab // rows, 3 * rows, count), f32),
        in_specs=[vmem] * 5,
        out_specs=vmem,
        scratch_shapes=[pltpu.VMEM((32, slab), f32)],
        compiler_params=pltpu.CompilerParams(vmem_limit_bytes=16 * 2**20),
        cost_estimate=pl.CostEstimate(flops=10**9, bytes_accessed=8 * 10**6, transcendentals=0),
        name="gate_pack",
    )(projected, halo, taps, filters, jnp.asarray(spread_table()))


def conv_kernel(rows, width, skip, x, e_in, tw, c_in, c_out, e_out, out, feat):
    cos, sin = tw[:, :BLK], tw[:, BLK:]

    def load(i, c):
        return x[pl.ds(i * rows + c, BLK, stride=3 * rows), :]

    def step(it, carry):
        chans = [it * width + j for j in range(width)]
        gates = []
        pieces = []
        for c in chans:
            gate = load(0, c)
            gates.append(gate)
            pieces += [gate, load(1, c)]
        hi, lo = split(jnp.concatenate(pieces, axis=1))
        s = dot(e_in[...], jnp.concatenate([hi, lo, hi], axis=0))
        turned = []
        for j in range(2 * width):
            sr = s[:BLK, j * BLK : (j + 1) * BLK]
            si = s[BLK:, j * BLK : (j + 1) * BLK]
            turned.append(jnp.concatenate([sr * cos - si * sin, sr * sin + si * cos], axis=1))
        hi, lo = split(jnp.concatenate(turned, axis=0))
        spec = dot(jnp.concatenate([hi, lo, hi], axis=1), c_in[...])
        prods = []
        for j in range(width):
            g = spec[2 * j * BLK : (2 * j + 1) * BLK]
            h = spec[(2 * j + 1) * BLK : (2 * j + 2) * BLK]
            gr, gi, hr, hm = g[:, :BLK], g[:, BLK:], h[:, :BLK], h[:, BLK:]
            prods.append(jnp.concatenate([gr * hr - gi * hm, gr * hm + gi * hr], axis=1))
        hi, lo = split(jnp.concatenate(prods, axis=0))
        v = dot(jnp.concatenate([hi, lo, hi], axis=1), c_out[...])
        us = []
        for j in range(width):
            vr, vi = v[j * BLK : (j + 1) * BLK, :BLK], v[j * BLK : (j + 1) * BLK, BLK:]
            us.append(jnp.concatenate([vr * cos + vi * sin, vi * cos - vr * sin], axis=0))
        hi, lo = split(jnp.concatenate(us, axis=1))
        y = dot(e_out[...], jnp.concatenate([hi, lo, hi], axis=0))
        for j, c in enumerate(chans):
            f = (y[:, j * BLK : (j + 1) * BLK] + skip[c] * gates[j]) * load(2, c)
            feat[pl.ds(c, BLK, stride=rows), :] = f
        return carry

    lax.fori_loop(0, rows // width, step, 0)
    done = feat[...].reshape(BLK, rows, BLK).astype(bf16)
    out[0] = done
    out[1] = done


def conv_features(x, skip, rows):
    vmem = pl.BlockSpec(memory_space=pltpu.VMEM)
    smem = pl.BlockSpec(memory_space=pltpu.SMEM)
    consts = [jnp.asarray(t) for t in tables()]
    return pl.pallas_call(
        lambda *refs: conv_kernel(rows, 8, *refs),
        out_shape=jax.ShapeDtypeStruct((2, BLK, rows, BLK), bf16),
        in_specs=[smem] + [vmem] * 6,
        out_specs=vmem,
        scratch_shapes=[pltpu.VMEM((BLK * rows, BLK), f32)],
        compiler_params=pltpu.CompilerParams(vmem_limit_bytes=20 * 2**20),
        cost_estimate=pl.CostEstimate(flops=4 * 10**9, bytes_accessed=6 * 10**6, transcendentals=0),
        name="conv_features",
    )(skip, x.reshape(BLK * 3 * rows, BLK), *consts)


def spread(w_out):
    wt = w_out.reshape(w_out.shape[0], -1).T
    parts = []
    for k in range(4):
        pairs = []
        for zs in range(4):
            for cs in range(2):
                i = (zs % 2) * 2 + cs
                pairs.append((zs * 2 + cs, ((i + k) % 4) * 2 + zs // 2))
        parts.append(lax.ppermute(wt, ("z", "core"), pairs))
    return parts


def proj_kernel(pos, own, other, w, out_own, out_other, acc):
    chips, parts, cols, depth = w.shape
    both = jnp.concatenate([own[...], other[...]], axis=1)
    for i in range(parts):
        k = lax.rem(pos[0] + 4 - i, 4)
        t = dot(w[:, k].reshape(chips * cols, depth), both)
        acc[i // 2, :, i % 2] = t.reshape(chips, cols, 2 * BLK)
    flat = acc[...].reshape(chips * parts * cols, 2 * BLK)
    for c in range(0, flat.shape[0], BLK):
        out_own[:, c : c + BLK] = flat[c : c + BLK, :BLK].T
        out_other[:, c : c + BLK] = flat[c : c + BLK, BLK:].T


def project(pos, own, other, w):
    vmem = pl.BlockSpec(memory_space=pltpu.VMEM)
    chips, parts, cols, depth = w.shape
    shape = jax.ShapeDtypeStruct((BLK, chips * parts * cols), f32)
    return pl.pallas_call(
        proj_kernel,
        out_shape=(shape, shape),
        in_specs=[pl.BlockSpec(memory_space=pltpu.SMEM), vmem, vmem, vmem],
        out_specs=(vmem, vmem),
        scratch_shapes=[pltpu.VMEM((2, chips, 2, cols, 2 * BLK), f32)],
        compiler_params=pltpu.CompilerParams(vmem_limit_bytes=24 * 2**20),
        name="project",
    )(pos, own, other, w)


def body(projected, short_taps, filters, skip_gain, w_out):
    slab, count = filters.shape
    groups = lax.axis_size(SEQ)
    rows = slab // groups
    me = lax.axis_index(SEQ)
    core = lax.axis_index("core")
    skip = lax.dynamic_slice(skip_gain, (me * rows,), (rows,)) / (G_SCALE * M_SCALE)
    last = edges(projected)
    last, w_out = lax.optimization_barrier((last, w_out))
    halo = lax.ppermute(last, SEQ, [(i, i + 1) for i in range(groups - 1)])
    parts = spread(w_out)
    taps = short_taps.transpose(0, 2, 1)
    packed = gate_pack(projected, halo, taps, filters, rows).astype(f16)
    packed, parts = lax.optimization_barrier((packed, parts))
    w = lax.all_gather(jnp.stack(parts), ("x", "y"))
    w = w.reshape(-1, 4, w.shape[-2], w.shape[-1])
    x = lax.all_to_all(packed, SEQ, split_axis=0, concat_axis=0, tiled=True)
    feats = conv_features(x.astype(f32), skip, rows).reshape(2 * groups, rows, count)
    mine = lax.all_to_all(feats, ("chan",) + SEQ, split_axis=0, concat_axis=0, tiled=True)
    mine = mine.reshape(2 * slab, count)
    mine, w = lax.optimization_barrier((mine, w))
    swap = [(0, 1), (1, 0)]
    other = lax.ppermute(mine, "core", swap)
    out_own, out_other = project(lax.axis_index("z").reshape(1), mine, other, w)
    got = lax.ppermute(out_other, "core", swap)
    return jnp.where(
        core == 0,
        jnp.concatenate([out_own, got], axis=1),
        jnp.concatenate([got, out_own], axis=1),
    )


def solution(mesh):
    fine = Mesh(mesh.devices.reshape(4, 4, 4, 2, 2), SEQ + ("chan",))
    in_specs = (
        P(None, "chan", SEQ),
        P(None, "chan", None),
        P("chan", SEQ),
        P("chan"),
        P(None, "chan", SEQ),
    )
    out_specs = P(SEQ, "chan")
    return jax.shard_map(body, mesh=fine, in_specs=in_specs, out_specs=out_specs, check_vma=False)
```

```python
import math

import jax
import jax.numpy as jnp
import numpy as np
import ml_dtypes
from jax import lax
from jax.experimental import pallas as pl
from jax.experimental.pallas import tpu as pltpu
from jax.sharding import Mesh, PartitionSpec as P

BLK = 128
SEQ = ("z", "x", "y", "core")
G_SCALE = 2.0 ** 3
M_SCALE = 2.0 ** 9
H_SCALE = 2.0 ** 15
f32 = jnp.float32
bf16 = jnp.bfloat16
f16 = jnp.float16


def split_np(m):
    hi = m.astype(np.float32).astype(ml_dtypes.bfloat16)
    lo = (m - hi.astype(np.float64)).astype(np.float32).astype(ml_dtypes.bfloat16)
    return hi, lo


def tables():
    n = BLK * BLK
    k1 = np.arange(BLK)[:, None] + 0.25
    a = np.arange(BLK)[None, :]
    alpha = 2.0 * np.pi * a * k1 / BLK
    fwd_rows = np.concatenate([np.cos(alpha), np.sin(alpha)], axis=0)
    hi, lo = split_np(fwd_rows)
    rows_in = np.concatenate([hi, hi, lo], axis=1)
    tw = 2.0 * np.pi * a * k1 / n
    twiddle = np.concatenate([np.cos(tw), np.sin(tw)], axis=1).astype(np.float32)
    beta = 2.0 * np.pi * ((np.arange(BLK)[:, None] * a) % BLK) / BLK
    c, s = np.cos(beta), np.sin(beta)
    hi, lo = split_np(np.block([[c, s], [-s, c]]))
    cols_in = np.concatenate([hi, hi, lo], axis=0)
    hi, lo = split_np(np.block([[c, -s], [s, c]]))
    cols_out = np.concatenate([hi, hi, lo], axis=0)
    back = np.concatenate([np.cos(alpha).T, np.sin(alpha).T], axis=1) / (n * H_SCALE * G_SCALE * M_SCALE)
    hi, lo = split_np(back)
    rows_out = np.concatenate([hi, hi, lo], axis=1)
    return rows_in, twiddle, cols_in, cols_out, rows_out


def split(x):
    hi = x.astype(bf16)
    lo = (x - hi.astype(f32)).astype(bf16)
    return hi, lo


def dot(a, b):
    return jnp.dot(a, b, preferred_element_type=f32)


def edge_kernel(p, out):
    lane = lax.broadcasted_iota(jnp.int32, (BLK, BLK), 1)
    for q in range(0, p.shape[1], BLK):
        x = [p[i, q : q + BLK, :] for i in range(3)]
        x = [pltpu.roll(x[0], BLK - 4, 1), pltpu.roll(x[1], BLK - 2, 1), x[2]]
        t = jnp.where(lane < BLK - 4, x[0], jnp.where(lane < BLK - 2, x[1], x[2]))
        out[:, q : q + BLK] = t.T[BLK - 8 :]


def edges(projected):
    vmem = pl.BlockSpec(memory_space=pltpu.VMEM)
    return pl.pallas_call(
        edge_kernel,
        out_shape=jax.ShapeDtypeStruct((8, projected.shape[1]), f32),
        in_specs=[vmem],
        out_specs=vmem,
        name="edges",
    )(projected)


def spread_table():
    e = np.zeros((32, 15, BLK), np.float32)
    for i in range(3):
        for j in range(3):
            e[8 + 8 * i + j, 3 * i + j, :] = 1.0
        e[2 * i + 3, 9 + i, 0] = 1.0
        e[2 * i + 2, 12 + i, 0] = 1.0
        e[2 * i + 3, 12 + i, 1] = 1.0
    e = e.reshape(32, 15 * BLK)
    return np.concatenate([e, e, e], axis=0).astype(ml_dtypes.bfloat16)


def gate_kernel(rows, p, halo, taps, h, table, out, left_ref):
    lane = lax.broadcasted_iota(jnp.int32, (BLK, BLK), 1)
    group = BLK // rows
    left_ref[0:8, :] = halo[...]
    left_ref[8:32, :] = jnp.zeros((24, left_ref.shape[1]), f32)
    for i in range(3):
        left_ref[8 + 8 * i : 11 + 8 * i, :] = taps[i]
    left = left_ref[...]
    parts = []
    for k in range(3):
        parts.append(left.astype(bf16))
        left = left - parts[-1].astype(f32)
    cols = jnp.concatenate(parts, axis=0)
    shape = (group, rows, BLK)
    for it in range(h.shape[0] // BLK):
        sl = slice(it * BLK, (it + 1) * BLK)
        wide = lax.dot_general(
            cols[:, sl], table[...], (((0,), (0,)), ((), ())), preferred_element_type=f32
        )
        col = [wide[:, j * BLK : (j + 1) * BLK] for j in range(15)]
        mixed = []
        for i in range(3):
            x = p[i, sl, :]
            x1 = jnp.where(lane < 1, col[9 + i], pltpu.roll(x, 1, 1))
            x2 = jnp.where(lane < 2, col[12 + i], pltpu.roll(x, 2, 1))
            mixed.append(col[3 * i] * x + col[3 * i + 1] * x1 + col[3 * i + 2] * x2)
        dst = slice(it * group, (it + 1) * group)
        out[dst, 0:rows, :] = (mixed[1] * mixed[2] * G_SCALE).reshape(shape)
        out[dst, rows : 2 * rows, :] = (h[sl, :] * H_SCALE).reshape(shape)
        out[dst, 2 * rows : 3 * rows, :] = (mixed[0] * M_SCALE).reshape(shape)


def gate_pack(projected, halo, taps, filters, rows):
    slab, count = filters.shape
    vmem = pl.BlockSpec(memory_space=pltpu.VMEM)
    return pl.pallas_call(
        lambda *refs: gate_kernel(rows, *refs),
        out_shape=jax.ShapeDtypeStruct((slab // rows, 3 * rows, count), f32),
        in_specs=[vmem] * 5,
        out_specs=vmem,
        scratch_shapes=[pltpu.VMEM((32, slab), f32)],
        compiler_params=pltpu.CompilerParams(vmem_limit_bytes=16 * 2**20),
        cost_estimate=pl.CostEstimate(flops=8 * 10**9, bytes_accessed=8 * 10**6, transcendentals=0),
        name="gate_pack",
    )(projected, halo, taps, filters, jnp.asarray(spread_table()))


def conv_kernel(rows, width, skip, x, e_in, tw, c_in, c_out, e_out, out, feat):
    cos, sin = tw[:, :BLK], tw[:, BLK:]

    def load(i, c):
        return x[pl.ds(i * rows + c, BLK, stride=3 * rows), :]

    def step(it, carry):
        chans = [it * width + j for j in range(width)]
        gates = []
        pieces = []
        for c in chans:
            gate = load(0, c)
            gates.append(gate)
            pieces += [gate, load(1, c)]
        hi, lo = split(jnp.concatenate(pieces, axis=1))
        s = dot(e_in[...], jnp.concatenate([hi, lo, hi], axis=0))
        turned = []
        for j in range(2 * width):
            sr = s[:BLK, j * BLK : (j + 1) * BLK]
            si = s[BLK:, j * BLK : (j + 1) * BLK]
            turned.append(jnp.concatenate([sr * cos - si * sin, sr * sin + si * cos], axis=1))
        hi, lo = split(jnp.concatenate(turned, axis=0))
        spec = dot(jnp.concatenate([hi, lo, hi], axis=1), c_in[...])
        prods = []
        for j in range(width):
            g = spec[2 * j * BLK : (2 * j + 1) * BLK]
            h = spec[(2 * j + 1) * BLK : (2 * j + 2) * BLK]
            gr, gi, hr, hm = g[:, :BLK], g[:, BLK:], h[:, :BLK], h[:, BLK:]
            prods.append(jnp.concatenate([gr * hr - gi * hm, gr * hm + gi * hr], axis=1))
        hi, lo = split(jnp.concatenate(prods, axis=0))
        v = dot(jnp.concatenate([hi, lo, hi], axis=1), c_out[...])
        us = []
        for j in range(width):
            vr, vi = v[j * BLK : (j + 1) * BLK, :BLK], v[j * BLK : (j + 1) * BLK, BLK:]
            us.append(jnp.concatenate([vr * cos + vi * sin, vi * cos - vr * sin], axis=0))
        hi, lo = split(jnp.concatenate(us, axis=1))
        y = dot(e_out[...], jnp.concatenate([hi, lo, hi], axis=0))
        for j, c in enumerate(chans):
            f = (y[:, j * BLK : (j + 1) * BLK] + skip[c] * gates[j]) * load(2, c)
            feat[pl.ds(c, BLK, stride=rows), :] = f
        return carry

    lax.fori_loop(0, rows // width, step, 0)
    done = feat[...].reshape(BLK, rows, BLK).astype(bf16)
    out[0] = done
    out[1] = done


def conv_features(x, skip, rows):
    vmem = pl.BlockSpec(memory_space=pltpu.VMEM)
    smem = pl.BlockSpec(memory_space=pltpu.SMEM)
    consts = [jnp.asarray(t) for t in tables()]
    return pl.pallas_call(
        lambda *refs: conv_kernel(rows, 8, *refs),
        out_shape=jax.ShapeDtypeStruct((2, BLK, rows, BLK), bf16),
        in_specs=[smem] + [vmem] * 6,
        out_specs=vmem,
        scratch_shapes=[pltpu.VMEM((BLK * rows, BLK), f32)],
        compiler_params=pltpu.CompilerParams(vmem_limit_bytes=20 * 2**20),
        cost_estimate=pl.CostEstimate(flops=4 * 10**9, bytes_accessed=6 * 10**6, transcendentals=0),
        name="conv_features",
    )(skip, x.reshape(BLK * 3 * rows, BLK), *consts)


SWAP = [(0, 1), (1, 0)]


def chip_columns(w_out):
    wt = w_out.reshape(w_out.shape[0], -1).T
    return jnp.concatenate([wt, lax.ppermute(wt, "core", SWAP)], axis=0)


def spread(pair):
    parts = []
    for r in range(2):
        pairs = []
        for zs in range(4):
            for cs in range(2):
                pairs.append((zs * 2 + cs, ((zs + r) % 2 + 2 * cs) * 2 + zs // 2))
        parts.append(lax.ppermute(pair, ("z", "core"), pairs))
    return parts


def proj_kernel(pos, own, other, w, out_own, out_other, acc):
    chips, parts, cols, depth = w.shape
    both = jnp.concatenate([own[...], other[...]], axis=1)
    for i in range(parts):
        r, h = lax.rem(pos[0] + i // 2, 2), lax.rem(pos[0] // 2 + i % 2, 2)
        k = 2 * r + h
        t = dot(w[:, k].reshape(chips * cols, depth), both)
        acc[i // 2, :, i % 2] = t.reshape(chips, cols, 2 * BLK)
    flat = acc[...].reshape(chips * parts * cols, 2 * BLK)
    for c in range(0, flat.shape[0], BLK):
        out_own[:, c : c + BLK] = flat[c : c + BLK, :BLK].T
        out_other[:, c : c + BLK] = flat[c : c + BLK, BLK:].T


def project(pos, own, other, w):
    vmem = pl.BlockSpec(memory_space=pltpu.VMEM)
    chips, parts, cols, depth = w.shape
    shape = jax.ShapeDtypeStruct((BLK, chips * parts * cols), f32)
    return pl.pallas_call(
        proj_kernel,
        out_shape=(shape, shape),
        in_specs=[pl.BlockSpec(memory_space=pltpu.SMEM), vmem, vmem, vmem],
        out_specs=(vmem, vmem),
        scratch_shapes=[pltpu.VMEM((2, chips, 2, cols, 2 * BLK), f32)],
        compiler_params=pltpu.CompilerParams(vmem_limit_bytes=24 * 2**20),
        name="project",
    )(pos, own, other, w)


def body(projected, short_taps, filters, skip_gain, w_out):
    slab, count = filters.shape
    groups = lax.axis_size(SEQ)
    rows = slab // groups
    me = lax.axis_index(SEQ)
    core = lax.axis_index("core")
    skip = lax.dynamic_slice(skip_gain, (me * rows,), (rows,)) / (G_SCALE * M_SCALE)
    last = edges(projected)
    last, pair = lax.optimization_barrier((last, chip_columns(w_out)))
    halo = lax.ppermute(last, SEQ, [(i, i + 1) for i in range(groups - 1)])
    parts = spread(pair)
    taps = short_taps.transpose(0, 2, 1)
    packed = gate_pack(projected, halo, taps, filters, rows).astype(f16)
    packed, parts = lax.optimization_barrier((packed, parts))
    w = lax.all_gather(jnp.stack(parts), ("x", "y"))
    w = w.reshape(-1, 4, w.shape[-2] // 2, w.shape[-1])
    x = lax.all_to_all(packed, SEQ, split_axis=0, concat_axis=0, tiled=True)
    feats = conv_features(x.astype(f32), skip, rows).reshape(2 * groups, rows, count)
    mine = lax.all_to_all(feats, ("chan",) + SEQ, split_axis=0, concat_axis=0, tiled=True)
    mine = mine.reshape(2 * slab, count)
    mine, w = lax.optimization_barrier((mine, w))
    other = lax.ppermute(mine, "core", SWAP)
    out_own, out_other = project(lax.axis_index("z").reshape(1), mine, other, w)
    got = lax.ppermute(out_other, "core", SWAP)
    return jnp.where(
        core == 0,
        jnp.concatenate([out_own, got], axis=1),
        jnp.concatenate([got, out_own], axis=1),
    )


def solution(mesh):
    fine = Mesh(mesh.devices.reshape(4, 4, 4, 2, 2), SEQ + ("chan",))
    in_specs = (
        P(None, "chan", SEQ),
        P(None, "chan", None),
        P("chan", SEQ),
        P("chan"),
        P(None, "chan", SEQ),
    )
    out_specs = P(SEQ, "chan")
    return jax.shard_map(body, mesh=fine, in_specs=in_specs, out_specs=out_specs, check_vma=False)
```

```python
import math

import jax
import jax.numpy as jnp
import numpy as np
import ml_dtypes
from jax import lax
from jax.experimental import pallas as pl
from jax.experimental.pallas import tpu as pltpu
from jax.sharding import Mesh, PartitionSpec as P

BLK = 128
SEQ = ("z", "x", "y", "core")
G_SCALE = 2.0 ** 3
M_SCALE = 2.0 ** 9
H_SCALE = 2.0 ** 15
f32 = jnp.float32
bf16 = jnp.bfloat16
f16 = jnp.float16


def split_np(m):
    hi = m.astype(np.float32).astype(ml_dtypes.bfloat16)
    lo = (m - hi.astype(np.float64)).astype(np.float32).astype(ml_dtypes.bfloat16)
    return hi, lo


def tables():
    n = BLK * BLK
    k1 = np.arange(BLK)[:, None] + 0.25
    a = np.arange(BLK)[None, :]
    alpha = 2.0 * np.pi * a * k1 / BLK
    fwd_rows = np.concatenate([np.cos(alpha), np.sin(alpha)], axis=0)
    hi, lo = split_np(fwd_rows)
    rows_in = np.concatenate([hi, hi, lo], axis=1)
    tw = 2.0 * np.pi * a * k1 / n
    twiddle = np.concatenate([np.cos(tw), np.sin(tw)], axis=1).astype(np.float32)
    beta = 2.0 * np.pi * ((np.arange(BLK)[:, None] * a) % BLK) / BLK
    c, s = np.cos(beta), np.sin(beta)
    hi, lo = split_np(np.block([[c, s], [-s, c]]))
    cols_in = np.concatenate([hi, hi, lo], axis=0)
    hi, lo = split_np(np.block([[c, -s], [s, c]]))
    cols_out = np.concatenate([hi, hi, lo], axis=0)
    back = np.concatenate([np.cos(alpha).T, np.sin(alpha).T], axis=1) / (n * H_SCALE * G_SCALE * M_SCALE)
    hi, lo = split_np(back)
    rows_out = np.concatenate([hi, hi, lo], axis=1)
    return rows_in, twiddle, cols_in, cols_out, rows_out


def split(x):
    hi = x.astype(bf16)
    lo = (x - hi.astype(f32)).astype(bf16)
    return hi, lo


def dot(a, b):
    return jnp.dot(a, b, preferred_element_type=f32)


def edge_kernel(p, out, held, sems):
    lane = lax.broadcasted_iota(jnp.int32, (BLK, BLK), 1)
    parts = sems.shape[0]
    per = p.shape[1] // parts
    loads = []
    for n in range(parts):
        part = pl.ds(n * per, per)
        loads.append(pltpu.make_async_copy(p.at[:, part], held.at[:, part], sems.at[n]))
        loads[n].start()
    for n in range(parts):
        loads[n].wait()
        for q in range(n * per, (n + 1) * per, BLK):
            x = [held[i, q : q + BLK, :] for i in range(3)]
            x = [pltpu.roll(x[0], BLK - 4, 1), pltpu.roll(x[1], BLK - 2, 1), x[2]]
            t = jnp.where(lane < BLK - 4, x[0], jnp.where(lane < BLK - 2, x[1], x[2]))
            out[:, q : q + BLK] = t.T[BLK - 8 :]


def edges(projected):
    return pl.pallas_call(
        edge_kernel,
        out_shape=jax.ShapeDtypeStruct((8, projected.shape[1]), f32),
        in_specs=[pl.BlockSpec(memory_space=pl.ANY)],
        out_specs=pl.BlockSpec(memory_space=pltpu.VMEM),
        scratch_shapes=[pltpu.VMEM(projected.shape, f32), pltpu.SemaphoreType.DMA((8,))],
        compiler_params=pltpu.CompilerParams(vmem_limit_bytes=16 * 2**20),
        name="edges",
    )(projected)


def spread_table():
    e = np.zeros((32, 15, BLK), np.float32)
    for i in range(3):
        for j in range(3):
            e[8 + 8 * i + j, 3 * i + j, :] = 1.0
        e[2 * i + 3, 9 + i, 0] = 1.0
        e[2 * i + 2, 12 + i, 0] = 1.0
        e[2 * i + 3, 12 + i, 1] = 1.0
    e = e.reshape(32, 15 * BLK)
    return np.concatenate([e, e, e], axis=0).astype(ml_dtypes.bfloat16)


def gate_kernel(rows, p, halo, taps, h, table, out, left_ref):
    lane = lax.broadcasted_iota(jnp.int32, (BLK, BLK), 1)
    group = BLK // rows
    left_ref[0:8, :] = halo[...]
    left_ref[8:32, :] = jnp.zeros((24, left_ref.shape[1]), f32)
    for i in range(3):
        left_ref[8 + 8 * i : 11 + 8 * i, :] = taps[i]
    left = left_ref[...]
    parts = []
    for k in range(3):
        parts.append(left.astype(bf16))
        left = left - parts[-1].astype(f32)
    cols = jnp.concatenate(parts, axis=0)
    shape = (group, rows, BLK)
    for it in range(h.shape[0] // BLK):
        sl = slice(it * BLK, (it + 1) * BLK)
        wide = lax.dot_general(
            cols[:, sl], table[...], (((0,), (0,)), ((), ())), preferred_element_type=f32
        )
        col = [wide[:, j * BLK : (j + 1) * BLK] for j in range(15)]
        mixed = []
        for i in range(3):
            x = p[i, sl, :]
            x1 = jnp.where(lane < 1, col[9 + i], pltpu.roll(x, 1, 1))
            x2 = jnp.where(lane < 2, col[12 + i], pltpu.roll(x, 2, 1))
            mixed.append(col[3 * i] * x + col[3 * i + 1] * x1 + col[3 * i + 2] * x2)
        dst = slice(it * group, (it + 1) * group)
        out[dst, 0:rows, :] = (mixed[1] * mixed[2] * G_SCALE).reshape(shape)
        out[dst, rows : 2 * rows, :] = (h[sl, :] * H_SCALE).reshape(shape)
        out[dst, 2 * rows : 3 * rows, :] = (mixed[0] * M_SCALE).reshape(shape)


def gate_pack(projected, halo, taps, filters, rows):
    slab, count = filters.shape
    vmem = pl.BlockSpec(memory_space=pltpu.VMEM)
    return pl.pallas_call(
        lambda *refs: gate_kernel(rows, *refs),
        out_shape=jax.ShapeDtypeStruct((slab // rows, 3 * rows, count), f32),
        in_specs=[vmem] * 5,
        out_specs=vmem,
        scratch_shapes=[pltpu.VMEM((32, slab), f32)],
        compiler_params=pltpu.CompilerParams(vmem_limit_bytes=16 * 2**20),
        cost_estimate=pl.CostEstimate(flops=10**9, bytes_accessed=8 * 10**6, transcendentals=0),
        name="gate_pack",
    )(projected, halo, taps, filters, jnp.asarray(spread_table()))


def conv_kernel(rows, width, skip, x, e_in, tw, c_in, c_out, e_out, out, feat):
    cos, sin = tw[:, :BLK], tw[:, BLK:]

    def load(i, c):
        return x[pl.ds(i * rows + c, BLK, stride=3 * rows), :]

    def step(it, carry):
        chans = [it * width + j for j in range(width)]
        gates = []
        pieces = []
        for c in chans:
            gate = load(0, c)
            gates.append(gate)
            pieces += [gate, load(1, c)]
        hi, lo = split(jnp.concatenate(pieces, axis=1))
        s = dot(e_in[...], jnp.concatenate([hi, lo, hi], axis=0))
        turned = []
        for j in range(2 * width):
            sr = s[:BLK, j * BLK : (j + 1) * BLK]
            si = s[BLK:, j * BLK : (j + 1) * BLK]
            turned.append(jnp.concatenate([sr * cos - si * sin, sr * sin + si * cos], axis=1))
        hi, lo = split(jnp.concatenate(turned, axis=0))
        spec = dot(jnp.concatenate([hi, lo, hi], axis=1), c_in[...])
        prods = []
        for j in range(width):
            g = spec[2 * j * BLK : (2 * j + 1) * BLK]
            h = spec[(2 * j + 1) * BLK : (2 * j + 2) * BLK]
            gr, gi, hr, hm = g[:, :BLK], g[:, BLK:], h[:, :BLK], h[:, BLK:]
            prods.append(jnp.concatenate([gr * hr - gi * hm, gr * hm + gi * hr], axis=1))
        hi, lo = split(jnp.concatenate(prods, axis=0))
        v = dot(jnp.concatenate([hi, lo, hi], axis=1), c_out[...])
        us = []
        for j in range(width):
            vr, vi = v[j * BLK : (j + 1) * BLK, :BLK], v[j * BLK : (j + 1) * BLK, BLK:]
            us.append(jnp.concatenate([vr * cos + vi * sin, vi * cos - vr * sin], axis=0))
        hi, lo = split(jnp.concatenate(us, axis=1))
        y = dot(e_out[...], jnp.concatenate([hi, lo, hi], axis=0))
        for j, c in enumerate(chans):
            f = (y[:, j * BLK : (j + 1) * BLK] + skip[c] * gates[j]) * load(2, c)
            feat[pl.ds(c, BLK, stride=rows), :] = f
        return carry

    lax.fori_loop(0, rows // width, step, 0)
    done = feat[...].reshape(BLK, rows, BLK).astype(bf16)
    out[0] = done
    out[1] = done


def conv_features(x, skip, rows):
    vmem = pl.BlockSpec(memory_space=pltpu.VMEM)
    smem = pl.BlockSpec(memory_space=pltpu.SMEM)
    consts = [jnp.asarray(t) for t in tables()]
    return pl.pallas_call(
        lambda *refs: conv_kernel(rows, 8, *refs),
        out_shape=jax.ShapeDtypeStruct((2, BLK, rows, BLK), bf16),
        in_specs=[smem] + [vmem] * 6,
        out_specs=vmem,
        scratch_shapes=[pltpu.VMEM((BLK * rows, BLK), f32)],
        compiler_params=pltpu.CompilerParams(vmem_limit_bytes=20 * 2**20),
        cost_estimate=pl.CostEstimate(flops=4 * 10**9, bytes_accessed=6 * 10**6, transcendentals=0),
        name="conv_features",
    )(skip, x.reshape(BLK * 3 * rows, BLK), *consts)


SWAP = [(0, 1), (1, 0)]


def chip_columns(w_out):
    wt = w_out.reshape(w_out.shape[0], -1).T
    return jnp.concatenate([wt, lax.ppermute(wt, "core", SWAP)], axis=0)


def spread(pair):
    parts = []
    for r in range(2):
        pairs = []
        for zs in range(4):
            for cs in range(2):
                pairs.append((zs * 2 + cs, ((zs + r) % 2 + 2 * cs) * 2 + zs // 2))
        parts.append(lax.ppermute(pair, ("z", "core"), pairs))
    return parts


def proj_kernel(pos, own, other, w, out_own, out_other, acc):
    chips, parts, cols, depth = w.shape
    both = jnp.concatenate([own[...], other[...]], axis=1)
    for i in range(parts):
        r, h = lax.rem(pos[0] + i // 2, 2), lax.rem(pos[0] // 2 + i % 2, 2)
        k = 2 * r + h
        t = dot(w[:, k].reshape(chips * cols, depth), both)
        acc[i // 2, :, i % 2] = t.reshape(chips, cols, 2 * BLK)
    flat = acc[...].reshape(chips * parts * cols, 2 * BLK)
    for c in range(0, flat.shape[0], BLK):
        out_own[:, c : c + BLK] = flat[c : c + BLK, :BLK].T
        out_other[:, c : c + BLK] = flat[c : c + BLK, BLK:].T


def project(pos, own, other, w):
    vmem = pl.BlockSpec(memory_space=pltpu.VMEM)
    chips, parts, cols, depth = w.shape
    shape = jax.ShapeDtypeStruct((BLK, chips * parts * cols), f32)
    return pl.pallas_call(
        proj_kernel,
        out_shape=(shape, shape),
        in_specs=[pl.BlockSpec(memory_space=pltpu.SMEM), vmem, vmem, vmem],
        out_specs=(vmem, vmem),
        scratch_shapes=[pltpu.VMEM((2, chips, 2, cols, 2 * BLK), f32)],
        compiler_params=pltpu.CompilerParams(vmem_limit_bytes=24 * 2**20),
        name="project",
    )(pos, own, other, w)


def body(projected, short_taps, filters, skip_gain, w_out):
    slab, count = filters.shape
    groups = lax.axis_size(SEQ)
    rows = slab // groups
    me = lax.axis_index(SEQ)
    core = lax.axis_index("core")
    skip = lax.dynamic_slice(skip_gain, (me * rows,), (rows,)) / (G_SCALE * M_SCALE)
    last = edges(projected)
    pair = chip_columns(w_out)
    halo = lax.ppermute(last, SEQ, [(i, i + 1) for i in range(groups - 1)])
    parts = spread(pair)
    taps = short_taps.transpose(0, 2, 1)
    packed = gate_pack(projected, halo, taps, filters, rows).astype(f16)
    packed, parts = lax.optimization_barrier((packed, parts))
    w = lax.all_gather(jnp.stack(parts), ("x", "y"))
    w = w.reshape(-1, 4, w.shape[-2] // 2, w.shape[-1])
    x = lax.all_to_all(packed, SEQ, split_axis=0, concat_axis=0, tiled=True)
    feats = conv_features(x.astype(f32), skip, rows).reshape(2 * groups, rows, count)
    mine = lax.all_to_all(feats, ("chan",) + SEQ, split_axis=0, concat_axis=0, tiled=True)
    mine = mine.reshape(2 * slab, count)
    mine, w = lax.optimization_barrier((mine, w))
    other = lax.ppermute(mine, "core", SWAP)
    out_own, out_other = project(lax.axis_index("z").reshape(1), mine, other, w)
    got = lax.ppermute(out_other, "core", SWAP)
    return jnp.where(
        core == 0,
        jnp.concatenate([out_own, got], axis=1),
        jnp.concatenate([got, out_own], axis=1),
    )


def solution(mesh):
    fine = Mesh(mesh.devices.reshape(4, 4, 4, 2, 2), SEQ + ("chan",))
    in_specs = (
        P(None, "chan", SEQ),
        P(None, "chan", None),
        P("chan", SEQ),
        P("chan"),
        P(None, "chan", SEQ),
    )
    out_specs = P(SEQ, "chan")
    return jax.shard_map(body, mesh=fine, in_specs=in_specs, out_specs=out_specs, check_vma=False)
```
